32 devices in a mesh: groups: 2 (over x), hid: 16 (over z, y, core).
Axes of the slice: x: 2, y: 2, z: 4, core: 2. Of those that a mesh axis runs over, the one named last changes fastest.
Arguments:
- gate_pre: bfloat16 [1024, 49152], P('groups', 'hid'), parts along dimension 0, may hold values from -6 to 6
- up_pre: bfloat16 [1024, 49152], P('groups', 'hid'), parts along dimension 0, may hold values from -7 to 7
- down_weight: bfloat16 [49152, 8192], P('hid'), may hold values from -1 to 1
- residual: bfloat16 [1024, 8192], P('groups', 'hid'), parts along dimension 0, may hold values from -38 to 38
- norm_gain: bfloat16 [8192], P('hid'), may hold values from 0.5 to 1.5
Outputs:
- stream: bfloat16 [1024, 8192], P('groups', 'hid'), parts along dimension 0
- normed: bfloat16 [1024, 8192], P('groups', 'hid'), parts along dimension 0
The draws below stay inside these ranges and needn't reach their ends.
There are 2 independent parts, one for each index of `groups`. The reference program is written for one: setup_inputs(seed, part) draws one part's arguments, and reference() takes and returns one part's arrays. A program takes and returns all parts, laid end to end along the dimension named above; an argument that names none is the same for every part. Nothing has to cross between parts.
All inputs are finite; a program needn't handle non-finite values.
Results may differ from the reference program's by a relative error of at most 0.0031.
Values may be sent and summed in bfloat16 or wider, within the bound.
A program may use at most 192 MiB of HBM per device.

```python
import math
import jax
import jax.numpy as jnp
from jax import lax

D = 8192
FF = 49152
SPAN = 512


def draw_residual(key, part):
    key = jax.random.fold_in(key, 7)
    key_rows, key_cols, key_base = jax.random.split(key, 3)
    row_scale = jnp.exp(jax.random.uniform(key_rows, (SPAN, 1), jnp.float32) * math.log(10.0))
    ramp = jnp.exp(jnp.arange(D, dtype=jnp.float32) / D * math.log(3.0))
    col_scale = ramp[None, :] * jax.random.uniform(key_cols, (1, D), jnp.float32, 0.7, 1.4)
    base_noise = jnp.clip(jax.random.normal(key_base, (SPAN, D), jnp.float32), -6.0, 6.0)
    return (0.15 * row_scale * col_scale * base_noise).astype(jnp.bfloat16)


def draw_up_pre(key, part):
    key = jax.random.fold_in(key, 11)
    key_noise, key_sign, key_size = jax.random.split(key, 3)
    token_sign = jnp.where(jax.random.bernoulli(key_sign, 0.5, (SPAN, 1)), 1.0, -1.0).astype(jnp.float32)
    token_size = jax.random.uniform(key_size, (SPAN, 1), jnp.float32, 0.3, 0.8)
    noise_values = jnp.clip(jax.random.normal(key_noise, (SPAN, FF), jnp.float32), -6.0, 6.0)
    return (noise_values + token_sign * token_size).astype(jnp.bfloat16)


def draw_down_weight(key, part):
    key = jax.random.fold_in(key, 13)
    key_noise, key_rows, key_cols = jax.random.split(key, 3)
    noise_values = jnp.clip(jax.random.normal(key_noise, (FF, D), jnp.float32), -6.0, 6.0)
    row_part = jax.random.uniform(key_rows, (FF, 1), jnp.float32, 0.025, 0.075)
    col_part = jnp.clip(jax.random.normal(key_cols, (1, D), jnp.float32), -3.0, 3.0)
    return ((noise_values + row_part * col_part) * FF ** (-0.5)).astype(jnp.bfloat16)


def block_scale(key, dims, shards, least, largest):
    loudness, own = 1.0, jax.random.fold_in(key, 6)
    for dim, shards_of in shards:
        draws = jnp.exp(jax.random.uniform(jax.random.fold_in(own, dim), (shards_of,), jnp.float32, least / len(shards), largest / len(shards)))
        loudness = loudness * jnp.repeat(draws, dims[dim] // shards_of).reshape([-1 if axis == dim else 1 for axis in range(len(dims))])
    return loudness


def noise(stream_key, shape, spread, most, pieces=(), kind=jnp.bfloat16):
    result = spread * jax.random.normal(stream_key, shape, jnp.float32)
    if pieces:
        result = result * block_scale(stream_key, shape, pieces, -0.22, 0.18)
    return jnp.clip(result, -most, most).astype(kind)


def setup_inputs(seed: int = 0, part: int = 0) -> dict:
    key_list = jax.random.split(jax.random.key(seed), 6)
    own_keys = jax.random.split(jax.random.fold_in(key_list[5], part), 6)
    gate_pre = noise(own_keys[0], (SPAN, FF), 1.0, 6.0, ((1, 16),))
    up_pre = draw_up_pre(jax.random.fold_in(jax.random.fold_in(key_list[5], part), 71), part)
    down_weight = draw_down_weight(jax.random.fold_in(key_list[5], 71), part)
    residual = draw_residual(jax.random.fold_in(jax.random.fold_in(key_list[5], part), 71), part)
    norm_gain = jnp.clip(1.0 + 0.1 * jax.random.normal(key_list[4], (D,), jnp.float32), 0.5, 1.5).astype(jnp.bfloat16)
    return dict(gate_pre=gate_pre, up_pre=up_pre, down_weight=down_weight, residual=residual, norm_gain=norm_gain)


def reference(gate_pre, up_pre, down_weight, residual, norm_gain):
    gate_values = gate_pre.astype(jnp.float32)
    hidden = (jax.nn.silu(gate_values) * up_pre.astype(jnp.float32)).astype(jnp.bfloat16)
    branch = jnp.dot(hidden, down_weight, preferred_element_type=jnp.float32)
    combined = residual.astype(jnp.float32) + branch
    stream = combined.astype(jnp.bfloat16)
    mean_square = lax.optimization_barrier(jnp.mean(combined * combined, axis=1, keepdims=True))
    normed = (combined * lax.rsqrt(mean_square + 1e-05) * norm_gain.astype(jnp.float32)).astype(jnp.bfloat16)
    return (stream, normed)
```

```python
import functools

import jax
import jax.numpy as jnp
from jax import lax
from jax.experimental import pallas as pl
from jax.experimental.pallas import tpu as pltpu
from jax.sharding import PartitionSpec as P

MESH = pl.DeviceIdType.MESH
SLOTS = 3
LOADS = 8


def kernel(
    n, total_features,
    gate_hbm, up_hbm, weight_hbm, residual_ref, gain_ref,
    stream_ref, normed_ref,
    gate, up, hidden, weights, acc, combined,
    send_c, recv_c, send_y, recv_y, send_z, recv_z, stats,
    load_sem, weight_sem, c_send_sem, c_recv_sem, y_send_sem, y_recv_sem,
    z_send_sem, z_recv_sem, s_send_sem, s_recv_sem,
):
    nz = n // 4
    tokens, feats = residual_ref.shape
    me = lax.axis_index("hid")
    core = lax.rem(me, 2)
    row = lax.rem(lax.div(me, 2), 2)
    layer = lax.div(me, 4)
    sibling = me + 1 - 2 * core
    across = me + 2 - 4 * row
    steps = 4 * nz

    barrier = pltpu.get_barrier_semaphore()

    @pl.loop(1, n)
    def _(k):
        pl.semaphore_signal(
            barrier, inc=1, device_id={"hid": lax.rem(me + k, n)}, device_id_type=MESH
        )

    load_rows = tokens // LOADS

    def input_copies(i):
        rows = pl.ds(i * load_rows, load_rows)
        return (
            pltpu.make_async_copy(gate_hbm.at[rows], gate.at[rows], load_sem.at[0, i]),
            pltpu.make_async_copy(up_hbm.at[rows], up.at[rows], load_sem.at[1, i]),
        )

    def split(s):
        phase = s // (2 * nz)
        j = (s // 2) % nz
        own = s % 2
        return phase, j, own

    def weight_copy(s):
        phase, j, own = split(s)
        dest_z = lax.rem(layer + 1 + j, nz)
        dest_y = jnp.where(phase == 0, 1 - row, row)
        dest_c = jnp.where(own == 1, core, 1 - core)
        dest = (dest_z * 2 + dest_y) * 2 + dest_c
        slot = lax.rem(s, SLOTS)
        columns = pl.ds(pl.multiple_of(dest * feats, feats), feats)
        return pltpu.make_async_copy(
            weight_hbm.at[:, columns], weights.at[slot], weight_sem.at[slot]
        )

    for i in range(LOADS):
        for copy in input_copies(i):
            copy.start()
    for s in range(SLOTS - 1):
        weight_copy(jnp.int32(s)).start()

    for i in range(LOADS):
        for copy in input_copies(i):
            copy.wait()

        @pl.loop(0, load_rows // 16)
        def _(r):
            rows = pl.ds(pl.multiple_of(i * load_rows + r * 16, 16), 16)
            half = gate[rows, :].astype(jnp.float32) * 0.5
            silu = half + half * jnp.tanh(half)
            hidden[rows, :] = (silu * up[rows, :].astype(jnp.float32)).astype(jnp.bfloat16)

    pl.semaphore_wait(barrier, n - 1)

    def c_copy(i):
        return pltpu.make_async_remote_copy(
            src_ref=send_c.at[i], dst_ref=recv_c.at[i],
            send_sem=c_send_sem.at[i], recv_sem=c_recv_sem.at[i],
            device_id={"hid": sibling}, device_id_type=MESH,
        )

    def y_copy(j):
        return pltpu.make_async_remote_copy(
            src_ref=send_y.at[j], dst_ref=recv_y.at[j],
            send_sem=y_send_sem.at[j], recv_sem=y_recv_sem.at[j],
            device_id={"hid": across}, device_id_type=MESH,
        )

    def z_copy(j):
        return pltpu.make_async_remote_copy(
            src_ref=send_z.at[j], dst_ref=recv_z.at[j],
            send_sem=z_send_sem.at[j], recv_sem=z_recv_sem.at[j],
            device_id={"hid": lax.rem(me + 4 * (1 + j), n)}, device_id_type=MESH,
        )

    chunk = 64

    def by_rows(work):
        @pl.loop(0, tokens // chunk)
        def _(r):
            work(pl.ds(pl.multiple_of(r * chunk, chunk), chunk))

    f32 = jnp.float32

    @pl.loop(0, steps)
    def _(s):
        phase, j, own = split(s)
        weight_copy(s).wait()

        @pl.when(s + SLOTS - 1 < steps)
        def _():
            weight_copy(s + SLOTS - 1).start()

        acc[...] = jnp.dot(
            hidden[...], weights[lax.rem(s, SLOTS)], preferred_element_type=f32
        )
        at = phase * nz + j

        @pl.when(own == 0)
        def _():
            def work(rows):
                send_c[at, rows, :] = acc[rows, :].astype(jnp.bfloat16)

            by_rows(work)
            c_copy(at).start()

        @pl.when(own == 1)
        def _():
            c_copy(at).wait_recv()

            @pl.when(phase == 0)
            def _():
                def work(rows):
                    send_y[j, rows, :] = (
                        acc[rows, :] + recv_c[at, rows, :].astype(f32)
                    ).astype(jnp.bfloat16)

                by_rows(work)
                y_copy(j).start()

            @pl.when(phase == 1)
            def _():
                y_copy(j).wait_recv()

                @pl.when(j < nz - 1)
                def _():
                    def work(rows):
                        send_z[j, rows, :] = (
                            acc[rows, :] + recv_c[at, rows, :].astype(f32)
                            + recv_y[j, rows, :].astype(f32)
                        ).astype(jnp.bfloat16)

                    by_rows(work)
                    z_copy(j).start()

                @pl.when(j == nz - 1)
                def _():
                    def work(rows):
                        combined[rows, :] = (
                            acc[rows, :] + recv_c[at, rows, :].astype(f32)
                            + recv_y[j, rows, :].astype(f32)
                            + residual_ref[rows, :].astype(f32)
                        )

                    by_rows(work)

    @pl.loop(0, nz - 1)
    def _(j):
        z_copy(j).wait_recv()

        def work(rows):
            combined[rows, :] += recv_z[j, rows, :].astype(f32)

        by_rows(work)

    block = 128

    @pl.loop(0, tokens // block)
    def _(r):
        rows = pl.ds(pl.multiple_of(r * block, block), block)
        values = combined[rows, :]
        stream_ref[rows, :] = values.astype(jnp.bfloat16)
        squares = values * values
        folded = squares[:, 0:128]
        for f in range(1, feats // 128):
            folded += squares[:, f * 128:(f + 1) * 128]
        sums = jnp.sum(folded.T, axis=0, keepdims=True)
        stats[0, :, rows] = jnp.broadcast_to(sums, (8, block))

    def s_copy(k):
        return pltpu.make_async_remote_copy(
            src_ref=stats.at[0], dst_ref=stats.at[k],
            send_sem=s_send_sem.at[k], recv_sem=s_recv_sem.at[k],
            device_id={"hid": lax.rem(me + k, n)}, device_id_type=MESH,
        )

    @pl.loop(1, n)
    def _(k):
        s_copy(k).start()

    @pl.loop(1, n)
    def _(k):
        s_copy(k).wait_recv()

    gain = gain_ref[...].astype(f32)

    @pl.loop(0, tokens // block)
    def _(r):
        rows = pl.ds(pl.multiple_of(r * block, block), block)
        whole = stats[0, :, rows]
        for k in range(1, n):
            whole += stats[k, :, rows]
        scale = lax.rsqrt(whole / total_features + 1e-05)
        scale = jnp.broadcast_to(scale[0:1, :], (block, block)).T
        for f in range(feats // 128):
            cols = slice(f * 128, (f + 1) * 128)
            normed_ref[rows, cols] = (combined[rows, cols] * scale * gain[:, cols]).astype(
                jnp.bfloat16
            )

    @pl.loop(0, 2 * nz)
    def _(i):
        c_copy(i).wait_send()

    @pl.loop(0, nz)
    def _(j):
        y_copy(j).wait_send()

    @pl.loop(0, nz - 1)
    def _(j):
        z_copy(j).wait_send()

    @pl.loop(1, n)
    def _(k):
        s_copy(k).wait_send()


def body(n, gate_pre, up_pre, down_weight, residual, norm_gain):
    nz = n // 4
    tokens, depth = gate_pre.shape
    feats = residual.shape[1]
    bf16, f32 = jnp.bfloat16, jnp.float32
    dma = pltpu.SemaphoreType.DMA
    vmem = pl.BlockSpec(memory_space=pltpu.VMEM)
    hbm = pl.BlockSpec(memory_space=pl.ANY)
    out = jax.ShapeDtypeStruct((tokens, feats), bf16)
    return pl.pallas_call(
        functools.partial(kernel, n, down_weight.shape[1]),
        out_shape=(out, out),
        in_specs=[hbm, hbm, hbm, vmem, vmem],
        out_specs=(vmem, vmem),
        scratch_shapes=[
            pltpu.VMEM((tokens, depth), bf16),
            pltpu.VMEM((tokens, depth), bf16),
            pltpu.VMEM((tokens, depth), bf16),
            pltpu.VMEM((SLOTS, depth, feats), bf16),
            pltpu.VMEM((tokens, feats), f32),
            pltpu.VMEM((tokens, feats), f32),
            pltpu.VMEM((2 * nz, tokens, feats), bf16),
            pltpu.VMEM((2 * nz, tokens, feats), bf16),
            pltpu.VMEM((nz, tokens, feats), bf16),
            pltpu.VMEM((nz, tokens, feats), bf16),
            pltpu.VMEM((nz - 1, tokens, feats), bf16),
            pltpu.VMEM((nz - 1, tokens, feats), bf16),
            pltpu.VMEM((n, 8, tokens), f32),
            dma((2, LOADS)),
            dma((SLOTS,)),
            dma((2 * nz,)),
            dma((2 * nz,)),
            dma((nz,)),
            dma((nz,)),
            dma((nz - 1,)),
            dma((nz - 1,)),
            dma((n,)),
            dma((n,)),
        ],
        compiler_params=pltpu.CompilerParams(
            collective_id=0, has_side_effects=True, vmem_limit_bytes=56 * 2**20
        ),
        cost_estimate=pl.CostEstimate(
            flops=2 * tokens * depth * down_weight.shape[1],
            bytes_accessed=2 * depth * (down_weight.shape[1] + 2 * tokens),
            transcendentals=tokens * depth,
        ),
    )(gate_pre, up_pre, down_weight, residual, norm_gain.reshape(1, feats))


def solution(mesh):
    return jax.shard_map(
        functools.partial(body, mesh.shape["hid"]),
        mesh=mesh,
        in_specs=(
            P("groups", "hid"),
            P("groups", "hid"),
            P("hid", None),
            P("groups", "hid"),
            P("hid"),
        ),
        out_specs=(P("groups", "hid"), P("groups", "hid")),
        check_vma=False,
    )
```

```python
import functools

import jax
import jax.numpy as jnp
from jax import lax
from jax.experimental import pallas as pl
from jax.experimental.pallas import tpu as pltpu
from jax.sharding import PartitionSpec as P

MESH = pl.DeviceIdType.MESH
SLOTS = 3
LOADS = 8


def kernel(
    n, total_features,
    gate_hbm, up_hbm, weight_hbm, residual_ref,
    combined, scale_ref,
    gate, up, hidden, weights, acc,
    send_c, recv_c, send_y, recv_y, send_z, recv_z, stats,
    load_sem, weight_sem, c_send_sem, c_recv_sem, y_send_sem, y_recv_sem,
    z_send_sem, z_recv_sem, s_send_sem, s_recv_sem,
):
    nz = n // 4
    tokens, feats = residual_ref.shape
    me = lax.axis_index("hid")
    core = lax.rem(me, 2)
    row = lax.rem(lax.div(me, 2), 2)
    layer = lax.div(me, 4)
    sibling = me + 1 - 2 * core
    across = me + 2 - 4 * row
    steps = 4 * nz

    barrier = pltpu.get_barrier_semaphore()

    @pl.loop(1, n)
    def _(k):
        pl.semaphore_signal(
            barrier, inc=1, device_id={"hid": lax.rem(me + k, n)}, device_id_type=MESH
        )

    load_rows = tokens // LOADS

    def input_copies(i):
        rows = pl.ds(i * load_rows, load_rows)
        return (
            pltpu.make_async_copy(gate_hbm.at[rows], gate.at[rows], load_sem.at[0, i]),
            pltpu.make_async_copy(up_hbm.at[rows], up.at[rows], load_sem.at[1, i]),
        )

    def split(s):
        phase = s // (2 * nz)
        j = (s // 2) % nz
        own = s % 2
        return phase, j, own

    below, above = layer, nz - 1 - layer
    lone = jnp.abs(above - below)
    both = jnp.minimum(above, below)

    def target(j):
        m = j - lone
        alone = jnp.where(above >= below, nz - 1 - j, j)
        distance = both - m // 2
        paired = jnp.where(m % 2 == 0, layer + distance, layer - distance)
        return jnp.where(j < lone, alone, paired)

    def weight_copy(s):
        phase, j, own = split(s)
        dest_z = target(j)
        dest_y = jnp.where(phase == 0, 1 - row, row)
        dest_c = jnp.where(own == 1, core, 1 - core)
        dest = (dest_z * 2 + dest_y) * 2 + dest_c
        slot = lax.rem(s, SLOTS)
        columns = pl.ds(pl.multiple_of(dest * feats, feats), feats)
        return pltpu.make_async_copy(
            weight_hbm.at[:, columns], weights.at[slot], weight_sem.at[slot]
        )

    for i in range(LOADS):
        for copy in input_copies(i):
            copy.start()
    for s in range(SLOTS - 1):
        weight_copy(jnp.int32(s)).start()

    for i in range(LOADS):
        for copy in input_copies(i):
            copy.wait()

        @pl.loop(0, load_rows // 16)
        def _(r):
            rows = pl.ds(pl.multiple_of(i * load_rows + r * 16, 16), 16)
            half = gate[rows, :].astype(jnp.float32) * 0.5
            silu = half + half * jnp.tanh(half)
            hidden[rows, :] = (silu * up[rows, :].astype(jnp.float32)).astype(jnp.bfloat16)

    pl.semaphore_wait(barrier, n - 1)

    def c_copy(i):
        return pltpu.make_async_remote_copy(
            src_ref=send_c.at[i], dst_ref=recv_c.at[i],
            send_sem=c_send_sem.at[i], recv_sem=c_recv_sem.at[i],
            device_id={"hid": sibling}, device_id_type=MESH,
        )

    def y_copy(j):
        return pltpu.make_async_remote_copy(
            src_ref=send_y.at[j], dst_ref=recv_y.at[j],
            send_sem=y_send_sem.at[j], recv_sem=y_recv_sem.at[j],
            device_id={"hid": across}, device_id_type=MESH,
        )

    def z_copy(j, dest):
        up_way = dest > layer
        slot = jnp.where(dest == layer - 1, nz, dest)
        return pltpu.make_async_remote_copy(
            src_ref=send_z.at[j], dst_ref=recv_z.at[slot],
            send_sem=z_send_sem.at[j], recv_sem=z_recv_sem.at[slot],
            device_id={"hid": jnp.where(up_way, me + 4, me - 4)}, device_id_type=MESH,
        )

    def z_arrival(slot):
        return pltpu.make_async_remote_copy(
            src_ref=send_z.at[0], dst_ref=recv_z.at[slot],
            send_sem=z_send_sem.at[0], recv_sem=z_recv_sem.at[slot],
            device_id={"hid": sibling}, device_id_type=MESH,
        )

    chunk = 64

    def by_rows(work):
        @pl.loop(0, tokens // chunk)
        def _(r):
            work(pl.ds(pl.multiple_of(r * chunk, chunk), chunk))

    f32 = jnp.float32

    @pl.loop(0, steps)
    def _(s):
        phase, j, own = split(s)
        weight_copy(s).wait()

        @pl.when(s + SLOTS - 1 < steps)
        def _():
            weight_copy(s + SLOTS - 1).start()

        acc[...] = jnp.dot(
            hidden[...], weights[lax.rem(s, SLOTS)], preferred_element_type=f32
        )
        at = phase * nz + j

        @pl.when(own == 0)
        def _():
            def work(rows):
                send_c[at, rows, :] = acc[rows, :].astype(jnp.bfloat16)

            by_rows(work)
            c_copy(at).start()

        @pl.when(own == 1)
        def _():
            c_copy(at).wait_recv()

            @pl.when(phase == 0)
            def _():
                def work(rows):
                    send_y[j, rows, :] = (
                        acc[rows, :] + recv_c[at, rows, :].astype(f32)
                    ).astype(jnp.bfloat16)

                by_rows(work)
                y_copy(j).start()

            @pl.when(phase == 1)
            def _():
                y_copy(j).wait_recv()

                def base(rows):
                    return (
                        acc[rows, :] + recv_c[at, rows, :].astype(f32)
                        + recv_y[j, rows, :].astype(f32)
                    )

                @pl.when(j < nz - 1)
                def _():
                    dest = target(j)
                    first = jnp.where(dest > layer, layer == 0, layer == nz - 1)

                    @pl.when(first)
                    def _():
                        def work(rows):
                            send_z[j, rows, :] = base(rows).astype(jnp.bfloat16)

                        by_rows(work)

                    @pl.when(jnp.logical_not(first))
                    def _():
                        z_arrival(dest).wait_recv()

                        def work(rows):
                            send_z[j, rows, :] = (
                                base(rows) + recv_z[dest, rows, :].astype(f32)
                            ).astype(jnp.bfloat16)

                        by_rows(work)

                    z_copy(j, dest).start()

                @pl.when(j == nz - 1)
                def _():
                    def work(rows):
                        combined[rows, :] = base(rows) + residual_ref[rows, :].astype(f32)

                    by_rows(work)

    def add_arrival(slot):
        z_arrival(slot).wait_recv()

        def work(rows):
            combined[rows, :] += recv_z[slot, rows, :].astype(f32)

        by_rows(work)

    @pl.when(layer > 0)
    def _():
        add_arrival(layer)

    @pl.when(layer < nz - 1)
    def _():
        add_arrival(nz)

    block = 128

    @pl.loop(0, tokens // block)
    def _(r):
        rows = pl.ds(pl.multiple_of(r * block, block), block)
        values = combined[rows, :]
        squares = values * values
        folded = squares[:, 0:128]
        for f in range(1, feats // 128):
            folded += squares[:, f * 128:(f + 1) * 128]
        sums = jnp.sum(folded.T, axis=0, keepdims=True)
        stats[0, :, rows] = jnp.broadcast_to(sums, (8, block))

    def s_copy(k):
        return pltpu.make_async_remote_copy(
            src_ref=stats.at[0], dst_ref=stats.at[k],
            send_sem=s_send_sem.at[k], recv_sem=s_recv_sem.at[k],
            device_id={"hid": lax.rem(me + k, n)}, device_id_type=MESH,
        )

    @pl.loop(1, n)
    def _(k):
        s_copy(k).start()

    @pl.loop(1, n)
    def _(k):
        s_copy(k).wait_recv()

    @pl.loop(0, tokens // block)
    def _(r):
        rows = pl.ds(pl.multiple_of(r * block, block), block)
        whole = stats[0, :, rows]
        for k in range(1, n):
            whole += stats[k, :, rows]
        scale = lax.rsqrt(whole / total_features + 1e-05)
        scale_ref[rows, :] = jnp.broadcast_to(scale[0:1, :], (block, block)).T

    @pl.loop(0, 2 * nz)
    def _(i):
        c_copy(i).wait_send()

    @pl.loop(0, nz)
    def _(j):
        y_copy(j).wait_send()

    @pl.loop(0, nz - 1)
    def _(j):
        z_copy(j, target(j)).wait_send()

    @pl.loop(1, n)
    def _(k):
        s_copy(k).wait_send()


def body(n, gate_pre, up_pre, down_weight, residual, norm_gain):
    nz = n // 4
    tokens, depth = gate_pre.shape
    feats = residual.shape[1]
    bf16, f32 = jnp.bfloat16, jnp.float32
    dma = pltpu.SemaphoreType.DMA
    vmem = pl.BlockSpec(memory_space=pltpu.VMEM)
    hbm = pl.BlockSpec(memory_space=pl.ANY)
    combined, scale = pl.pallas_call(
        functools.partial(kernel, n, down_weight.shape[1]),
        out_shape=(
            jax.ShapeDtypeStruct((tokens, feats), f32),
            jax.ShapeDtypeStruct((tokens, 128), f32),
        ),
        in_specs=[hbm, hbm, hbm, vmem],
        out_specs=(vmem, vmem),
        scratch_shapes=[
            pltpu.VMEM((tokens, depth), bf16),
            pltpu.VMEM((tokens, depth), bf16),
            pltpu.VMEM((tokens, depth), bf16),
            pltpu.VMEM((SLOTS, depth, feats), bf16),
            pltpu.VMEM((tokens, feats), f32),
            pltpu.VMEM((2 * nz, tokens, feats), bf16),
            pltpu.VMEM((2 * nz, tokens, feats), bf16),
            pltpu.VMEM((nz, tokens, feats), bf16),
            pltpu.VMEM((nz, tokens, feats), bf16),
            pltpu.VMEM((nz - 1, tokens, feats), bf16),
            pltpu.VMEM((nz + 1, tokens, feats), bf16),
            pltpu.VMEM((n, 8, tokens), f32),
            dma((2, LOADS)),
            dma((SLOTS,)),
            dma((2 * nz,)),
            dma((2 * nz,)),
            dma((nz,)),
            dma((nz,)),
            dma((nz - 1,)),
            dma((nz + 1,)),
            dma((n,)),
            dma((n,)),
        ],
        compiler_params=pltpu.CompilerParams(
            collective_id=0, has_side_effects=True, vmem_limit_bytes=56 * 2**20
        ),
        cost_estimate=pl.CostEstimate(
            flops=2 * tokens * depth * down_weight.shape[1],
            bytes_accessed=2 * depth * (down_weight.shape[1] + 2 * tokens),
            transcendentals=tokens * depth,
        ),
    )(gate_pre, up_pre, down_weight, residual)
    normed = combined * scale[:, :1] * norm_gain.astype(f32)
    return combined.astype(bf16), normed.astype(bf16)


def solution(mesh):
    return jax.shard_map(
        functools.partial(body, mesh.shape["hid"]),
        mesh=mesh,
        in_specs=(
            P("groups", "hid"),
            P("groups", "hid"),
            P("hid", None),
            P("groups", "hid"),
            P("hid"),
        ),
        out_specs=(P("groups", "hid"), P("groups", "hid")),
        check_vma=False,
    )
```

```python
import functools

import jax
import jax.numpy as jnp
from jax import lax
from jax.experimental import pallas as pl
from jax.experimental.pallas import tpu as pltpu
from jax.sharding import PartitionSpec as P

MESH = pl.DeviceIdType.MESH
SLOTS = 3
LOADS = 8


def kernel(
    n, total_features,
    gate_hbm, up_hbm, weight_hbm, residual_ref,
    combined, scale_ref,
    gate, up, hidden, weights, acc, kept,
    send_c, recv_c, send_y, recv_y, send_z, recv_z, stats,
    load_sem, weight_sem, c_send_sem, c_recv_sem, y_send_sem, y_recv_sem,
    z_send_sem, z_recv_sem, s_send_sem, s_recv_sem,
):
    nz = n // 4
    tokens, feats = residual_ref.shape
    me = lax.axis_index("hid")
    core = lax.rem(me, 2)
    row = lax.rem(lax.div(me, 2), 2)
    layer = lax.div(me, 4)
    sibling = me + 1 - 2 * core
    across = me + 2 - 4 * row
    steps = 4 * nz

    barrier = pltpu.get_barrier_semaphore()

    @pl.loop(1, n)
    def _(k):
        pl.semaphore_signal(
            barrier, inc=1, device_id={"hid": lax.rem(me + k, n)}, device_id_type=MESH
        )

    load_rows = tokens // LOADS

    def input_copies(i):
        rows = pl.ds(i * load_rows, load_rows)
        return (
            pltpu.make_async_copy(gate_hbm.at[rows], gate.at[rows], load_sem.at[0, i]),
            pltpu.make_async_copy(up_hbm.at[rows], up.at[rows], load_sem.at[1, i]),
        )

    def split(s):
        phase = (s // 2) % 2
        j = s // 4
        own = s % 2
        return phase, j, own

    below, above = layer, nz - 1 - layer
    lone = jnp.abs(above - below)
    both = jnp.minimum(above, below)

    def target(j):
        m = j - lone
        alone = jnp.where(above >= below, nz - 1 - j, j)
        distance = both - m // 2
        paired = jnp.where(m % 2 == 0, layer + distance, layer - distance)
        return jnp.where(j < lone, alone, paired)

    def weight_copy(s):
        phase, j, own = split(s)
        dest_z = target(j)
        dest_y = jnp.where(phase == 0, 1 - row, row)
        dest_c = jnp.where(own == 1, core, 1 - core)
        dest = (dest_z * 2 + dest_y) * 2 + dest_c
        slot = lax.rem(s, SLOTS)
        columns = pl.ds(pl.multiple_of(dest * feats, feats), feats)
        return pltpu.make_async_copy(
            weight_hbm.at[:, columns], weights.at[slot], weight_sem.at[slot]
        )

    for i in range(LOADS):
        for copy in input_copies(i):
            copy.start()
    for s in range(SLOTS - 1):
        weight_copy(jnp.int32(s)).start()

    for i in range(LOADS):
        for copy in input_copies(i):
            copy.wait()

        @pl.loop(0, load_rows // 16)
        def _(r):
            rows = pl.ds(pl.multiple_of(i * load_rows + r * 16, 16), 16)
            half = gate[rows, :].astype(jnp.float32) * 0.5
            silu = half + half * jnp.tanh(half)
            hidden[rows, :] = (silu * up[rows, :].astype(jnp.float32)).astype(jnp.bfloat16)

    pl.semaphore_wait(barrier, n - 1)

    def c_copy(i):
        return pltpu.make_async_remote_copy(
            src_ref=send_c.at[i], dst_ref=recv_c.at[i],
            send_sem=c_send_sem.at[i], recv_sem=c_recv_sem.at[i],
            device_id={"hid": sibling}, device_id_type=MESH,
        )

    def y_copy(j):
        return pltpu.make_async_remote_copy(
            src_ref=send_y.at[j], dst_ref=recv_y.at[j],
            send_sem=y_send_sem.at[j], recv_sem=y_recv_sem.at[j],
            device_id={"hid": across}, device_id_type=MESH,
        )

    def z_copy(j, dest):
        up_way = dest > layer
        slot = jnp.where(dest == layer - 1, nz, dest)
        return pltpu.make_async_remote_copy(
            src_ref=send_z.at[j], dst_ref=recv_z.at[slot],
            send_sem=z_send_sem.at[j], recv_sem=z_recv_sem.at[slot],
            device_id={"hid": jnp.where(up_way, me + 4, me - 4)}, device_id_type=MESH,
        )

    def z_arrival(slot):
        return pltpu.make_async_remote_copy(
            src_ref=send_z.at[0], dst_ref=recv_z.at[slot],
            send_sem=z_send_sem.at[0], recv_sem=z_recv_sem.at[slot],
            device_id={"hid": sibling}, device_id_type=MESH,
        )

    chunk = 64

    def by_rows(work):
        @pl.loop(0, tokens // chunk)
        def _(r):
            work(pl.ds(pl.multiple_of(r * chunk, chunk), chunk))

    f32 = jnp.float32

    def base(j, rows):
        return (
            kept[j % 2, rows, :] + recv_c[nz + j, rows, :].astype(f32)
            + recv_y[j, rows, :].astype(f32)
        )

    def arrive(j):
        c_copy(nz + j).wait_recv()
        y_copy(j).wait_recv()

    def pass_on(j):
        arrive(j)
        dest = target(j)
        first = jnp.where(dest > layer, layer == 0, layer == nz - 1)

        @pl.when(first)
        def _():
            def work(rows):
                send_z[j, rows, :] = base(j, rows).astype(jnp.bfloat16)

            by_rows(work)

        @pl.when(jnp.logical_not(first))
        def _():
            z_arrival(dest).wait_recv()

            def work(rows):
                send_z[j, rows, :] = (
                    base(j, rows) + recv_z[dest, rows, :].astype(f32)
                ).astype(jnp.bfloat16)

            by_rows(work)

        z_copy(j, dest).start()

    @pl.loop(0, steps)
    def _(s):
        phase, j, own = split(s)
        weight_copy(s).wait()

        @pl.when(s + SLOTS - 1 < steps)
        def _():
            weight_copy(s + SLOTS - 1).start()

        acc[...] = jnp.dot(
            hidden[...], weights[lax.rem(s, SLOTS)], preferred_element_type=f32
        )
        at = phase * nz + j

        @pl.when(own == 0)
        def _():
            def work(rows):
                send_c[at, rows, :] = acc[rows, :].astype(jnp.bfloat16)

            by_rows(work)
            c_copy(at).start()

        @pl.when((own == 1) & (phase == 0))
        def _():
            c_copy(at).wait_recv()

            def work(rows):
                send_y[j, rows, :] = (
                    acc[rows, :] + recv_c[at, rows, :].astype(f32)
                ).astype(jnp.bfloat16)

            by_rows(work)
            y_copy(j).start()

        @pl.when((own == 1) & (phase == 1))
        def _():
            def work(rows):
                kept[j % 2, rows, :] = acc[rows, :]

            by_rows(work)

            @pl.when(j > 0)
            def _():
                pass_on(j - 1)

    arrive(nz - 1)

    def last(rows):
        combined[rows, :] = base(nz - 1, rows) + residual_ref[rows, :].astype(f32)

    by_rows(last)

    def add_arrival(slot):
        z_arrival(slot).wait_recv()

        def work(rows):
            combined[rows, :] += recv_z[slot, rows, :].astype(f32)

        by_rows(work)

    @pl.when(layer > 0)
    def _():
        add_arrival(layer)

    @pl.when(layer < nz - 1)
    def _():
        add_arrival(nz)

    block = 128

    @pl.loop(0, tokens // block)
    def _(r):
        rows = pl.ds(pl.multiple_of(r * block, block), block)
        values = combined[rows, :]
        squares = values * values
        folded = squares[:, 0:128]
        for f in range(1, feats // 128):
            folded += squares[:, f * 128:(f + 1) * 128]
        sums = jnp.sum(folded.T, axis=0, keepdims=True)
        stats[0, :, rows] = jnp.broadcast_to(sums, (8, block))

    def s_copy(k):
        return pltpu.make_async_remote_copy(
            src_ref=stats.at[0], dst_ref=stats.at[k],
            send_sem=s_send_sem.at[k], recv_sem=s_recv_sem.at[k],
            device_id={"hid": lax.rem(me + k, n)}, device_id_type=MESH,
        )

    @pl.loop(1, n)
    def _(k):
        s_copy(k).start()

    @pl.loop(1, n)
    def _(k):
        s_copy(k).wait_recv()

    @pl.loop(0, tokens // block)
    def _(r):
        rows = pl.ds(pl.multiple_of(r * block, block), block)
        whole = stats[0, :, rows]
        for k in range(1, n):
            whole += stats[k, :, rows]
        scale = lax.rsqrt(whole / total_features + 1e-05)
        scale_ref[rows, :] = jnp.broadcast_to(scale[0:1, :], (block, block)).T

    @pl.loop(0, 2 * nz)
    def _(i):
        c_copy(i).wait_send()

    @pl.loop(0, nz)
    def _(j):
        y_copy(j).wait_send()

    @pl.loop(0, nz - 1)
    def _(j):
        z_copy(j, target(j)).wait_send()

    @pl.loop(1, n)
    def _(k):
        s_copy(k).wait_send()


def body(n, gate_pre, up_pre, down_weight, residual, norm_gain):
    nz = n // 4
    tokens, depth = gate_pre.shape
    feats = residual.shape[1]
    bf16, f32 = jnp.bfloat16, jnp.float32
    dma = pltpu.SemaphoreType.DMA
    vmem = pl.BlockSpec(memory_space=pltpu.VMEM)
    hbm = pl.BlockSpec(memory_space=pl.ANY)
    combined, scale = pl.pallas_call(
        functools.partial(kernel, n, down_weight.shape[1]),
        out_shape=(
            jax.ShapeDtypeStruct((tokens, feats), f32),
            jax.ShapeDtypeStruct((tokens, 128), f32),
        ),
        in_specs=[hbm, hbm, hbm, vmem],
        out_specs=(vmem, vmem),
        scratch_shapes=[
            pltpu.VMEM((tokens, depth), bf16),
            pltpu.VMEM((tokens, depth), bf16),
            pltpu.VMEM((tokens, depth), bf16),
            pltpu.VMEM((SLOTS, depth, feats), bf16),
            pltpu.VMEM((tokens, feats), f32),
            pltpu.VMEM((2, tokens, feats), f32),
            pltpu.VMEM((2 * nz, tokens, feats), bf16),
            pltpu.VMEM((2 * nz, tokens, feats), bf16),
            pltpu.VMEM((nz, tokens, feats), bf16),
            pltpu.VMEM((nz, tokens, feats), bf16),
            pltpu.VMEM((nz - 1, tokens, feats), bf16),
            pltpu.VMEM((nz + 1, tokens, feats), bf16),
            pltpu.VMEM((n, 8, tokens), f32),
            dma((2, LOADS)),
            dma((SLOTS,)),
            dma((2 * nz,)),
            dma((2 * nz,)),
            dma((nz,)),
            dma((nz,)),
            dma((nz - 1,)),
            dma((nz + 1,)),
            dma((n,)),
            dma((n,)),
        ],
        compiler_params=pltpu.CompilerParams(
            collective_id=0, has_side_effects=True, vmem_limit_bytes=56 * 2**20
        ),
        cost_estimate=pl.CostEstimate(
            flops=2 * tokens * depth * down_weight.shape[1],
            bytes_accessed=2 * depth * (down_weight.shape[1] + 2 * tokens),
            transcendentals=tokens * depth,
        ),
    )(gate_pre, up_pre, down_weight, residual)
    normed = combined * scale[:, :1] * norm_gain.astype(f32)
    return combined.astype(bf16), normed.astype(bf16)


def solution(mesh):
    return jax.shard_map(
        functools.partial(body, mesh.shape["hid"]),
        mesh=mesh,
        in_specs=(
            P("groups", "hid"),
            P("groups", "hid"),
            P("hid", None),
            P("groups", "hid"),
            P("hid"),
        ),
        out_specs=(P("groups", "hid"), P("groups", "hid")),
        check_vma=False,
    )
```

```python
import functools

import jax
import jax.numpy as jnp
from jax import lax
from jax.experimental import pallas as pl
from jax.experimental.pallas import tpu as pltpu
from jax.sharding import PartitionSpec as P

MESH = pl.DeviceIdType.MESH
SLOTS = 3
HALVES = 2
LOADS = 8


def kernel(
    n, total_features,
    gate_hbm, up_hbm, weight_hbm, residual_ref,
    combined, scale_ref,
    gate, up, hidden, weights, acc, kept,
    send_c, recv_c, send_y, recv_y, send_z, recv_z, stats,
    load_sem, weight_sem, c_send_sem, c_recv_sem, y_send_sem, y_recv_sem,
    z_send_sem, z_recv_sem, s_send_sem, s_recv_sem,
):
    nz = n // 4
    tokens, feats = residual_ref.shape
    me = lax.axis_index("hid")
    core = lax.rem(me, 2)
    row = lax.rem(lax.div(me, 2), 2)
    layer = lax.div(me, 4)
    sibling = me + 1 - 2 * core
    across = me + 2 - 4 * row
    steps = 4 * nz

    barrier = pltpu.get_barrier_semaphore()

    @pl.loop(1, n)
    def _(k):
        pl.semaphore_signal(
            barrier, inc=1, device_id={"hid": lax.rem(me + k, n)}, device_id_type=MESH
        )

    load_rows = tokens // LOADS

    def input_copies(i):
        rows = pl.ds(i * load_rows, load_rows)
        return (
            pltpu.make_async_copy(gate_hbm.at[rows], gate.at[rows], load_sem.at[0, i]),
            pltpu.make_async_copy(up_hbm.at[rows], up.at[rows], load_sem.at[1, i]),
        )

    def split(s):
        phase = (s // 2) % 2
        j = s // 4
        own = s % 2
        return phase, j, own

    below, above = layer, nz - 1 - layer
    lone = jnp.abs(above - below)
    both = jnp.minimum(above, below)

    def target(j):
        m = j - lone
        alone = jnp.where(above >= below, nz - 1 - j, j)
        distance = both - m // 2
        paired = jnp.where(m % 2 == 0, layer + distance, layer - distance)
        return jnp.where(j < lone, alone, paired)

    def weight_copy(s):
        phase, j, own = split(s)
        dest_z = target(j)
        dest_y = jnp.where(phase == 0, 1 - row, row)
        dest_c = jnp.where(own == 1, core, 1 - core)
        dest = (dest_z * 2 + dest_y) * 2 + dest_c
        slot = lax.rem(s, SLOTS)
        columns = pl.ds(pl.multiple_of(dest * feats, feats), feats)
        return pltpu.make_async_copy(
            weight_hbm.at[:, columns], weights.at[slot], weight_sem.at[slot]
        )

    for i in range(LOADS):
        for copy in input_copies(i):
            copy.start()
    for s in range(SLOTS - 1):
        weight_copy(jnp.int32(s)).start()

    for i in range(LOADS):
        for copy in input_copies(i):
            copy.wait()

        @pl.loop(0, load_rows // 16)
        def _(r):
            rows = pl.ds(pl.multiple_of(i * load_rows + r * 16, 16), 16)
            half = gate[rows, :].astype(jnp.float32) * 0.5
            silu = half + half * jnp.tanh(half)
            hidden[rows, :] = (silu * up[rows, :].astype(jnp.float32)).astype(jnp.bfloat16)

    pl.semaphore_wait(barrier, n - 1)

    def c_copy(i):
        return pltpu.make_async_remote_copy(
            src_ref=send_c.at[i], dst_ref=recv_c.at[i],
            send_sem=c_send_sem.at[i], recv_sem=c_recv_sem.at[i],
            device_id={"hid": sibling}, device_id_type=MESH,
        )

    half_rows = tokens // HALVES

    def y_copy(j, h):
        part = pl.ds(h * half_rows, half_rows)
        return pltpu.make_async_remote_copy(
            src_ref=send_y.at[j, part], dst_ref=recv_y.at[j, part],
            send_sem=y_send_sem.at[j, h], recv_sem=y_recv_sem.at[j, h],
            device_id={"hid": across}, device_id_type=MESH,
        )

    def z_copy(j, dest, h):
        part = pl.ds(h * half_rows, half_rows)
        up_way = dest > layer
        slot = jnp.where(dest == layer - 1, nz, dest)
        return pltpu.make_async_remote_copy(
            src_ref=send_z.at[j, part], dst_ref=recv_z.at[slot, part],
            send_sem=z_send_sem.at[j, h], recv_sem=z_recv_sem.at[slot, h],
            device_id={"hid": jnp.where(up_way, me + 4, me - 4)}, device_id_type=MESH,
        )

    def z_arrival(slot, h):
        part = pl.ds(h * half_rows, half_rows)
        return pltpu.make_async_remote_copy(
            src_ref=send_z.at[0, part], dst_ref=recv_z.at[slot, part],
            send_sem=z_send_sem.at[0, h], recv_sem=z_recv_sem.at[slot, h],
            device_id={"hid": sibling}, device_id_type=MESH,
        )

    chunk = 64

    def by_rows(work, h=None):
        first, count = (0, tokens) if h is None else (h * half_rows, half_rows)

        @pl.loop(first // chunk, (first + count) // chunk)
        def _(r):
            work(pl.ds(pl.multiple_of(r * chunk, chunk), chunk))

    f32 = jnp.float32

    def base(j, rows):
        return (
            kept[j % 2, rows, :] + recv_c[nz + j, rows, :].astype(f32)
            + recv_y[j, rows, :].astype(f32)
        )

    def arrive(j, h):
        if h == 0:
            c_copy(nz + j).wait_recv()
        y_copy(j, h).wait_recv()

    def pass_on(j, h):
        arrive(j, h)
        dest = target(j)
        first = jnp.where(dest > layer, layer == 0, layer == nz - 1)

        @pl.when(first)
        def _():
            def work(rows):
                send_z[j, rows, :] = base(j, rows).astype(jnp.bfloat16)

            by_rows(work, h)

        @pl.when(jnp.logical_not(first))
        def _():
            z_arrival(dest, h).wait_recv()

            def work(rows):
                send_z[j, rows, :] = (
                    base(j, rows) + recv_z[dest, rows, :].astype(f32)
                ).astype(jnp.bfloat16)

            by_rows(work, h)

        z_copy(j, dest, h).start()

    @pl.loop(0, steps)
    def _(s):
        phase, j, own = split(s)
        weight_copy(s).wait()

        @pl.when(s + SLOTS - 1 < steps)
        def _():
            weight_copy(s + SLOTS - 1).start()

        acc[...] = jnp.dot(
            hidden[...], weights[lax.rem(s, SLOTS)], preferred_element_type=f32
        )
        at = phase * nz + j

        @pl.when(own == 0)
        def _():
            def work(rows):
                send_c[at, rows, :] = acc[rows, :].astype(jnp.bfloat16)

            by_rows(work)
            c_copy(at).start()

        @pl.when((own == 1) & (phase == 0))
        def _():
            c_copy(at).wait_recv()

            def work(rows):
                send_y[j, rows, :] = (
                    acc[rows, :] + recv_c[at, rows, :].astype(f32)
                ).astype(jnp.bfloat16)

            for h in range(HALVES):
                by_rows(work, h)
                y_copy(j, h).start()

            @pl.when(j > 0)
            def _():
                pass_on(j - 1, 0)

        @pl.when((own == 1) & (phase == 1))
        def _():
            def work(rows):
                kept[j % 2, rows, :] = acc[rows, :]

            by_rows(work)

            @pl.when(j > 0)
            def _():
                pass_on(j - 1, 1)


    def last(rows):
        combined[rows, :] = base(nz - 1, rows) + residual_ref[rows, :].astype(f32)

    for h in range(HALVES):
        arrive(nz - 1, h)
        by_rows(last, h)

    def add_arrival(slot):
        def work(rows):
            combined[rows, :] += recv_z[slot, rows, :].astype(f32)

        for h in range(HALVES):
            z_arrival(slot, h).wait_recv()
            by_rows(work, h)

    @pl.when(layer > 0)
    def _():
        add_arrival(layer)

    @pl.when(layer < nz - 1)
    def _():
        add_arrival(nz)

    block = 128

    @pl.loop(0, tokens // block)
    def _(r):
        rows = pl.ds(pl.multiple_of(r * block, block), block)
        values = combined[rows, :]
        squares = values * values
        folded = squares[:, 0:128]
        for f in range(1, feats // 128):
            folded += squares[:, f * 128:(f + 1) * 128]
        sums = jnp.sum(folded.T, axis=0, keepdims=True)
        stats[0, :, rows] = sums

    def s_copy(k):
        return pltpu.make_async_remote_copy(
            src_ref=stats.at[0], dst_ref=stats.at[k],
            send_sem=s_send_sem.at[k], recv_sem=s_recv_sem.at[k],
            device_id={"hid": lax.rem(me + k, n)}, device_id_type=MESH,
        )

    @pl.loop(1, n)
    def _(k):
        s_copy(k).start()

    @pl.loop(1, n)
    def _(k):
        s_copy(k).wait_recv()

    @pl.loop(0, tokens // block)
    def _(r):
        rows = pl.ds(pl.multiple_of(r * block, block), block)
        whole = stats[0, :, rows]
        for k in range(1, n):
            whole += stats[k, :, rows]
        scale = lax.rsqrt(whole / total_features + 1e-05)
        scale_ref[rows, :] = jnp.broadcast_to(scale, (block, block)).T

    @pl.loop(0, 2 * nz)
    def _(i):
        c_copy(i).wait_send()

    @pl.loop(0, nz)
    def _(j):
        for h in range(HALVES):
            y_copy(j, h).wait_send()

    @pl.loop(0, nz - 1)
    def _(j):
        for h in range(HALVES):
            z_copy(j, target(j), h).wait_send()

    @pl.loop(1, n)
    def _(k):
        s_copy(k).wait_send()


def body(n, gate_pre, up_pre, down_weight, residual, norm_gain):
    nz = n // 4
    tokens, depth = gate_pre.shape
    feats = residual.shape[1]
    bf16, f32 = jnp.bfloat16, jnp.float32
    dma = pltpu.SemaphoreType.DMA
    vmem = pl.BlockSpec(memory_space=pltpu.VMEM)
    hbm = pl.BlockSpec(memory_space=pl.ANY)
    combined, scale = pl.pallas_call(
        functools.partial(kernel, n, down_weight.shape[1]),
        out_shape=(
            jax.ShapeDtypeStruct((tokens, feats), f32),
            jax.ShapeDtypeStruct((tokens, 128), f32),
        ),
        in_specs=[hbm, hbm, hbm, vmem],
        out_specs=(vmem, vmem),
        scratch_shapes=[
            pltpu.VMEM((tokens, depth), bf16),
            pltpu.VMEM((tokens, depth), bf16),
            pltpu.VMEM((tokens, depth), bf16),
            pltpu.VMEM((SLOTS, depth, feats), bf16),
            pltpu.VMEM((tokens, feats), f32),
            pltpu.VMEM((2, tokens, feats), f32),
            pltpu.VMEM((2 * nz, tokens, feats), bf16),
            pltpu.VMEM((2 * nz, tokens, feats), bf16),
            pltpu.VMEM((nz, tokens, feats), bf16),
            pltpu.VMEM((nz, tokens, feats), bf16),
            pltpu.VMEM((nz - 1, tokens, feats), bf16),
            pltpu.VMEM((nz + 1, tokens, feats), bf16),
            pltpu.VMEM((n, 1, tokens), f32),
            dma((2, LOADS)),
            dma((SLOTS,)),
            dma((2 * nz,)),
            dma((2 * nz,)),
            dma((nz, HALVES)),
            dma((nz, HALVES)),
            dma((nz - 1, HALVES)),
            dma((nz + 1, HALVES)),
            dma((n,)),
            dma((n,)),
        ],
        compiler_params=pltpu.CompilerParams(
            collective_id=0, has_side_effects=True, vmem_limit_bytes=56 * 2**20
        ),
        cost_estimate=pl.CostEstimate(
            flops=2 * tokens * depth * down_weight.shape[1],
            bytes_accessed=2 * depth * (down_weight.shape[1] + 2 * tokens),
            transcendentals=tokens * depth,
        ),
    )(gate_pre, up_pre, down_weight, residual)
    normed = combined * scale[:, :1] * norm_gain.astype(f32)
    return combined.astype(bf16), normed.astype(bf16)


def solution(mesh):
    return jax.shard_map(
        functools.partial(body, mesh.shape["hid"]),
        mesh=mesh,
        in_specs=(
            P("groups", "hid"),
            P("groups", "hid"),
            P("hid", None),
            P("groups", "hid"),
            P("hid"),
        ),
        out_specs=(P("groups", "hid"), P("groups", "hid")),
        check_vma=False,
    )
```

```python
import functools

import jax
import jax.numpy as jnp
from jax import lax
from jax.experimental import pallas as pl
from jax.experimental.pallas import tpu as pltpu
from jax.sharding import PartitionSpec as P

MESH = pl.DeviceIdType.MESH
SLOTS = 3
PIECES = 4
LOADS = 8


def kernel(
    n, total_features,
    gate_hbm, up_hbm, weight_hbm, residual_ref,
    combined, scale_ref,
    gate, up, hidden, weights, acc, kept,
    send_c, recv_c, send_y, recv_y, send_z, recv_z, stats,
    load_sem, weight_sem, c_send_sem, c_recv_sem, y_send_sem, y_recv_sem,
    z_send_sem, z_recv_sem, s_send_sem, s_recv_sem,
):
    nz = n // 4
    tokens, feats = residual_ref.shape
    me = lax.axis_index("hid")
    core = lax.rem(me, 2)
    row = lax.rem(lax.div(me, 2), 2)
    layer = lax.div(me, 4)
    sibling = me + 1 - 2 * core
    across = me + 2 - 4 * row
    steps = 4 * nz

    barrier = pltpu.get_barrier_semaphore()

    @pl.loop(1, n)
    def _(k):
        pl.semaphore_signal(
            barrier, inc=1, device_id={"hid": lax.rem(me + k, n)}, device_id_type=MESH
        )

    load_rows = tokens // LOADS

    def input_copies(i):
        rows = pl.ds(i * load_rows, load_rows)
        return (
            pltpu.make_async_copy(gate_hbm.at[rows], gate.at[rows], load_sem.at[0, i]),
            pltpu.make_async_copy(up_hbm.at[rows], up.at[rows], load_sem.at[1, i]),
        )

    def split(s):
        phase = (s // 2) % 2
        j = s // 4
        own = s % 2
        return phase, j, own

    below, above = layer, nz - 1 - layer
    lone = jnp.abs(above - below)
    both = jnp.minimum(above, below)

    def target(j):
        m = j - lone
        alone = jnp.where(above >= below, nz - 1 - j, j)
        distance = both - m // 2
        paired = jnp.where(m % 2 == 0, layer + distance, layer - distance)
        return jnp.where(j < lone, alone, paired)

    def weight_copy(s):
        phase, j, own = split(s)
        dest_z = target(j)
        dest_y = jnp.where(phase == 0, 1 - row, row)
        dest_c = jnp.where(own == 1, core, 1 - core)
        dest = (dest_z * 2 + dest_y) * 2 + dest_c
        slot = lax.rem(s, SLOTS)
        columns = pl.ds(pl.multiple_of(dest * feats, feats), feats)
        return pltpu.make_async_copy(
            weight_hbm.at[:, columns], weights.at[slot], weight_sem.at[slot]
        )

    for i in range(LOADS):
        for copy in input_copies(i):
            copy.start()
    for s in range(SLOTS - 1):
        weight_copy(jnp.int32(s)).start()

    for i in range(LOADS):
        for copy in input_copies(i):
            copy.wait()

        @pl.loop(0, load_rows // 16)
        def _(r):
            rows = pl.ds(pl.multiple_of(i * load_rows + r * 16, 16), 16)
            half = gate[rows, :].astype(jnp.float32) * 0.5
            silu = half + half * jnp.tanh(half)
            hidden[rows, :] = (silu * up[rows, :].astype(jnp.float32)).astype(jnp.bfloat16)

    pl.semaphore_wait(barrier, n - 1)

    def c_copy(i):
        return pltpu.make_async_remote_copy(
            src_ref=send_c.at[i], dst_ref=recv_c.at[i],
            send_sem=c_send_sem.at[i], recv_sem=c_recv_sem.at[i],
            device_id={"hid": sibling}, device_id_type=MESH,
        )

    piece_rows = tokens // PIECES

    def y_copy(j, h):
        part = pl.ds(h * piece_rows, piece_rows)
        return pltpu.make_async_remote_copy(
            src_ref=send_y.at[j, part], dst_ref=recv_y.at[j, part],
            send_sem=y_send_sem.at[j, h], recv_sem=y_recv_sem.at[j, h],
            device_id={"hid": across}, device_id_type=MESH,
        )

    def z_copy(j, dest, h):
        part = pl.ds(h * piece_rows, piece_rows)
        up_way = dest > layer
        slot = jnp.where(dest == layer - 1, nz, dest)
        return pltpu.make_async_remote_copy(
            src_ref=send_z.at[j, part], dst_ref=recv_z.at[slot, part],
            send_sem=z_send_sem.at[j, h], recv_sem=z_recv_sem.at[slot, h],
            device_id={"hid": jnp.where(up_way, me + 4, me - 4)}, device_id_type=MESH,
        )

    def z_arrival(slot, h):
        part = pl.ds(h * piece_rows, piece_rows)
        return pltpu.make_async_remote_copy(
            src_ref=send_z.at[0, part], dst_ref=recv_z.at[slot, part],
            send_sem=z_send_sem.at[0, h], recv_sem=z_recv_sem.at[slot, h],
            device_id={"hid": sibling}, device_id_type=MESH,
        )

    chunk = 64

    def by_rows(work, h=None):
        first, count = (0, tokens) if h is None else (h * piece_rows, piece_rows)

        @pl.loop(first // chunk, (first + count) // chunk)
        def _(r):
            work(pl.ds(pl.multiple_of(r * chunk, chunk), chunk))

    f32 = jnp.float32

    def base(j, rows):
        return (
            kept[j % 2, rows, :] + recv_c[nz + j, rows, :].astype(f32)
            + recv_y[j, rows, :].astype(f32)
        )

    def arrive(j, h):
        if h == 0:
            c_copy(nz + j).wait_recv()
        y_copy(j, h).wait_recv()

    def pass_on(j, h):
        arrive(j, h)
        dest = target(j)
        first = jnp.where(dest > layer, layer == 0, layer == nz - 1)

        @pl.when(first)
        def _():
            def work(rows):
                send_z[j, rows, :] = base(j, rows).astype(jnp.bfloat16)

            by_rows(work, h)

        @pl.when(jnp.logical_not(first))
        def _():
            z_arrival(dest, h).wait_recv()

            def work(rows):
                send_z[j, rows, :] = (
                    base(j, rows) + recv_z[dest, rows, :].astype(f32)
                ).astype(jnp.bfloat16)

            by_rows(work, h)

        z_copy(j, dest, h).start()

    @pl.loop(0, steps)
    def _(s):
        phase, j, own = split(s)
        weight_copy(s).wait()

        @pl.when(s + SLOTS - 1 < steps)
        def _():
            weight_copy(s + SLOTS - 1).start()

        acc[...] = jnp.dot(
            hidden[...], weights[lax.rem(s, SLOTS)], preferred_element_type=f32
        )
        at = phase * nz + j

        @pl.when(own == 0)
        def _():
            def work(rows):
                send_c[at, rows, :] = acc[rows, :].astype(jnp.bfloat16)

            by_rows(work)
            c_copy(at).start()

        @pl.when((own == 1) & (phase == 0))
        def _():
            c_copy(at).wait_recv()

            def work(rows):
                send_y[j, rows, :] = (
                    acc[rows, :] + recv_c[at, rows, :].astype(f32)
                ).astype(jnp.bfloat16)

            for h in range(PIECES):
                by_rows(work, h)
                y_copy(j, h).start()

            @pl.when(j > 0)
            def _():
                for h in range(PIECES // 2):
                    pass_on(j - 1, h)

        @pl.when((own == 1) & (phase == 1))
        def _():
            def work(rows):
                kept[j % 2, rows, :] = acc[rows, :]

            by_rows(work)

            @pl.when(j > 0)
            def _():
                for h in range(PIECES // 2, PIECES):
                    pass_on(j - 1, h)


    def last(rows):
        combined[rows, :] = base(nz - 1, rows) + residual_ref[rows, :].astype(f32)

    for h in range(PIECES):
        arrive(nz - 1, h)
        by_rows(last, h)

    def add_arrival(slot):
        def work(rows):
            combined[rows, :] += recv_z[slot, rows, :].astype(f32)

        for h in range(PIECES):
            z_arrival(slot, h).wait_recv()
            by_rows(work, h)

    @pl.when(layer > 0)
    def _():
        add_arrival(layer)

    @pl.when(layer < nz - 1)
    def _():
        add_arrival(nz)

    block = 128

    @pl.loop(0, tokens // block)
    def _(r):
        rows = pl.ds(pl.multiple_of(r * block, block), block)
        values = combined[rows, :]
        squares = values * values
        folded = squares[:, 0:128]
        for f in range(1, feats // 128):
            folded += squares[:, f * 128:(f + 1) * 128]
        sums = jnp.sum(folded.T, axis=0, keepdims=True)
        stats[0, :, rows] = sums

    def s_copy(k):
        return pltpu.make_async_remote_copy(
            src_ref=stats.at[0], dst_ref=stats.at[k],
            send_sem=s_send_sem.at[k], recv_sem=s_recv_sem.at[k],
            device_id={"hid": lax.rem(me + k, n)}, device_id_type=MESH,
        )

    @pl.loop(1, n)
    def _(k):
        s_copy(k).start()

    @pl.loop(1, n)
    def _(k):
        s_copy(k).wait_recv()

    @pl.loop(0, tokens // block)
    def _(r):
        rows = pl.ds(pl.multiple_of(r * block, block), block)
        whole = stats[0, :, rows]
        for k in range(1, n):
            whole += stats[k, :, rows]
        scale = lax.rsqrt(whole / total_features + 1e-05)
        scale_ref[rows, :] = jnp.broadcast_to(scale, (block, block)).T

    @pl.loop(0, 2 * nz)
    def _(i):
        c_copy(i).wait_send()

    @pl.loop(0, nz)
    def _(j):
        for h in range(PIECES):
            y_copy(j, h).wait_send()

    @pl.loop(0, nz - 1)
    def _(j):
        for h in range(PIECES):
            z_copy(j, target(j), h).wait_send()

    @pl.loop(1, n)
    def _(k):
        s_copy(k).wait_send()


def body(n, gate_pre, up_pre, down_weight, residual, norm_gain):
    nz = n // 4
    tokens, depth = gate_pre.shape
    feats = residual.shape[1]
    bf16, f32 = jnp.bfloat16, jnp.float32
    dma = pltpu.SemaphoreType.DMA
    vmem = pl.BlockSpec(memory_space=pltpu.VMEM)
    hbm = pl.BlockSpec(memory_space=pl.ANY)
    combined, scale = pl.pallas_call(
        functools.partial(kernel, n, down_weight.shape[1]),
        out_shape=(
            jax.ShapeDtypeStruct((tokens, feats), f32),
            jax.ShapeDtypeStruct((tokens, 128), f32),
        ),
        in_specs=[hbm, hbm, hbm, vmem],
        out_specs=(vmem, vmem),
        scratch_shapes=[
            pltpu.VMEM((tokens, depth), bf16),
            pltpu.VMEM((tokens, depth), bf16),
            pltpu.VMEM((tokens, depth), bf16),
            pltpu.VMEM((SLOTS, depth, feats), bf16),
            pltpu.VMEM((tokens, feats), f32),
            pltpu.VMEM((2, tokens, feats), f32),
            pltpu.VMEM((2 * nz, tokens, feats), bf16),
            pltpu.VMEM((2 * nz, tokens, feats), bf16),
            pltpu.VMEM((nz, tokens, feats), bf16),
            pltpu.VMEM((nz, tokens, feats), bf16),
            pltpu.VMEM((nz - 1, tokens, feats), bf16),
            pltpu.VMEM((nz + 1, tokens, feats), bf16),
            pltpu.VMEM((n, 1, tokens), f32),
            dma((2, LOADS)),
            dma((SLOTS,)),
            dma((2 * nz,)),
            dma((2 * nz,)),
            dma((nz, PIECES)),
            dma((nz, PIECES)),
            dma((nz - 1, PIECES)),
            dma((nz + 1, PIECES)),
            dma((n,)),
            dma((n,)),
        ],
        compiler_params=pltpu.CompilerParams(
            collective_id=0, has_side_effects=True, vmem_limit_bytes=56 * 2**20
        ),
        cost_estimate=pl.CostEstimate(
            flops=2 * tokens * depth * down_weight.shape[1],
            bytes_accessed=2 * depth * (down_weight.shape[1] + 2 * tokens),
            transcendentals=tokens * depth,
        ),
    )(gate_pre, up_pre, down_weight, residual)
    normed = combined * scale[:, :1] * norm_gain.astype(f32)
    return combined.astype(bf16), normed.astype(bf16)


def solution(mesh):
    return jax.shard_map(
        functools.partial(body, mesh.shape["hid"]),
        mesh=mesh,
        in_specs=(
            P("groups", "hid"),
            P("groups", "hid"),
            P("hid", None),
            P("groups", "hid"),
            P("hid"),
        ),
        out_specs=(P("groups", "hid"), P("groups", "hid")),
        check_vma=False,
    )
```
